32 devices in a mesh: groups: 2 (over y), rows: 4 (over z), cols: 2 (over x), sub: 2 (over core).
Axes of the slice: x: 2, y: 2, z: 4, core: 2. Of those that a mesh axis runs over, the one named last changes fastest.
Arguments:
- library: bfloat16 [81920, 1024], P(('groups', 'rows', 'cols', 'sub')), parts along dimension 0, as said below
- pick_order: int32 [512], P('groups'), parts along dimension 0, may hold values from 0 to 40959, as said below
Outputs:
- centered: bfloat16 [4, 128, 40960], P('groups', ('rows', 'cols', 'sub')), parts along dimension 0
The draws below stay inside these ranges and needn't reach their ends.
There are 2 independent parts, one for each index of `groups`. The reference program is written for one: setup_inputs(seed, part) draws one part's arguments, and reference() takes and returns one part's arrays. A program takes and returns all parts, laid end to end along the dimension named above; each array names one. Nothing has to cross between parts.
Inputs may be any that keep to these rules, and one draw needn't show every extreme that they name: `library`: every entry is at least 0.02. `pick_order`: the 256 picks are distinct library rows.
All inputs are finite; a program needn't handle non-finite values.
Results may differ from the reference program's by a relative error of at most 0.0063.
Values may be sent and summed in bfloat16 or wider, within the bound.
A program may use at most 64 MiB of HBM per device.

```python
import jax
import jax.numpy as jnp
from jax import lax

FEATURES = 1024
BLOCK = 128
BLOCKS = 2
LIBRARY = 40960
PICKS = 256


def draw_library(key, part):
    key_normal = jax.random.fold_in(key, 11)
    key_mask = jax.random.fold_in(key, 12)
    normal_part = jax.random.normal(key_normal, (LIBRARY, FEATURES), dtype=jnp.float32)
    uniform_part = jax.random.uniform(key_mask, (LIBRARY, FEATURES), dtype=jnp.float32)
    values = jnp.where(uniform_part < 0.4, jnp.exp(0.8 * normal_part), 0.0) + 0.02
    return values.astype(jnp.bfloat16)


def draw_pick_order(key, part):
    key_rows = jax.random.fold_in(key, 21)
    key_order = jax.random.fold_in(key, 22)
    middle = 1 + jax.random.permutation(key_rows, LIBRARY - 2)[:PICKS - 2]
    extremes = jnp.array([0, LIBRARY - 1], dtype=jnp.int32)
    joined = jnp.concatenate([extremes, middle.astype(jnp.int32)])
    return joined[jax.random.permutation(key_order, PICKS)].astype(jnp.int32)


def setup_inputs(seed: int = 0, part: int = 0) -> dict:
    keys = jax.random.split(jax.random.key(seed), 3)
    part_splits = jax.random.split(jax.random.fold_in(keys[2], part), 3)
    return {
        "library": draw_library(jax.random.fold_in(jax.random.fold_in(keys[2], part), 71), part),
        "pick_order": draw_pick_order(jax.random.fold_in(jax.random.fold_in(keys[2], part), 71), part),
    }


nugget = 0.1

def tanimoto(products, left_sq, right_sq):
    return products / (left_sq[:, None] + right_sq[None, :] - products)

def reference(library, pick_order):
    library_rows = library.shape[0]
    squares = jnp.sum(jnp.square(library.astype(jnp.float32)), axis=1)
    row_ids = jnp.arange(library_rows, dtype=jnp.int32)
    identity = jnp.eye(BLOCK, dtype=jnp.float32)
    factor_panel = None
    for block_id in range(BLOCKS):
        chosen = pick_order[block_id * BLOCK:(block_id + 1) * BLOCK]
        pick_rows = library[chosen]
        pick_squares = squares[chosen]
        products = jnp.dot(pick_rows.astype(jnp.float32), library.T.astype(jnp.float32), preferred_element_type=jnp.float32)
        marker = (chosen[:, None] == row_ids[None, :]).astype(jnp.float32)
        residual = tanimoto(products, pick_squares, squares) + nugget * marker
        pick_products = jnp.dot(pick_rows.astype(jnp.float32), pick_rows.T.astype(jnp.float32), preferred_element_type=jnp.float32)
        pivot_block = tanimoto(pick_products, pick_squares, pick_squares) + nugget * identity
        if block_id > 0:
            prior_rows = jnp.transpose(factor_panel[:, chosen])
            residual = residual - jnp.dot(prior_rows, factor_panel, precision=lax.Precision.HIGHEST)
            pivot_block = pivot_block - jnp.dot(prior_rows, prior_rows.T, precision=lax.Precision.HIGHEST)
        cholesky_low = jnp.linalg.cholesky(pivot_block)
        inverse = lax.linalg.triangular_solve(cholesky_low, identity, left_side=True, lower=True)
        new_panel = jnp.dot(inverse, residual, precision=lax.Precision.HIGHEST)
        factor_panel = new_panel if block_id == 0 else jnp.concatenate([factor_panel, new_panel], axis=0)
    rounded = lax.optimization_barrier(factor_panel.astype(jnp.bfloat16))
    values = rounded.astype(jnp.float32)
    column_mean = jnp.mean(values, axis=1, keepdims=True)
    centered = (values - column_mean).astype(jnp.bfloat16)
    return centered.reshape(BLOCKS, BLOCK, library_rows)
```

```python
import functools

import jax
import jax.numpy as jnp
from jax import lax
from jax.experimental import pallas as pl
from jax.experimental.pallas import tpu as pltpu
from jax.sharding import PartitionSpec as P

BLOCK = 128
BLOCKS = 2
GROUP = 16
SPREAD = ("rows", "cols", "sub")
MESH = pl.DeviceIdType.MESH
HIGHEST = lax.Precision.HIGHEST

nugget = 0.1


def tanimoto(products, left_sq, right_sq):
    return products / (left_sq[:, None] + right_sq[None, :] - products)


def pick_table(library, local_picks, owned_mask):
    clipped = jnp.clip(local_picks, 0, library.shape[0] - 1)
    taken = jnp.take(library, clipped, axis=0).astype(jnp.float32)
    return taken * owned_mask[:, None]


def regroup(block_panel):
    block_count, local_rows = block_panel.shape
    devices_all = lax.axis_size(SPREAD)
    shaped = block_panel.reshape(devices_all, block_count // devices_all, 1, local_rows)
    moved = lax.all_to_all(shaped, SPREAD, split_axis=0, concat_axis=2, tiled=True)
    return moved


def center_rows(moved, owned_count):
    values = moved.reshape(owned_count, -1).astype(jnp.float32)
    column_mean = jnp.mean(values, axis=1, keepdims=True)
    return (values - column_mean).astype(jnp.bfloat16)


def exchange_stages(sizes):
    stages = []
    for axis in ("sub", "cols", "rows"):
        bit = 1
        while bit < sizes[axis]:
            stages.append((axis, bit))
            bit *= 2
    return stages


def flipped(axis, bit):
    index = lax.axis_index(axis)
    high = lax.rem(index // bit, 2)
    return index + bit - 2 * bit * high, high


def gather_kernel(stages, local_ref, library_ref, out_ref, table, *rest):
    count = len(stages)
    landing = rest[:count]
    send_sem, recv_sem = rest[count:]
    barrier = pltpu.get_barrier_semaphore()
    partners = []
    for axis, bit in stages:
        other, high = flipped(axis, bit)
        partners.append((axis, other, high))
        pl.semaphore_signal(barrier, inc=1, device_id={axis: other}, device_id_type=MESH)
    picks, features = table.shape
    rows = library_ref.shape[0]
    hot = (local_ref[...] == lax.broadcasted_iota(jnp.int32, (picks, rows), 1)).astype(jnp.bfloat16)
    tile = 256
    for start in range(0, features, tile):
        table[:, start : start + tile] = jnp.dot(
            hot, library_ref[:, start : start + tile], preferred_element_type=jnp.float32
        ).astype(jnp.bfloat16)
    pl.semaphore_wait(barrier, count)
    base = 0
    size = picks
    bases = []
    for step, (axis, other, high) in enumerate(partners):
        size //= 2
        keep = pl.multiple_of(base + high * size, 16)
        give = pl.multiple_of(base + (1 - high) * size, 16)
        copy = pltpu.make_async_remote_copy(
            src_ref=table.at[pl.ds(give, size)],
            dst_ref=landing[step],
            send_sem=send_sem.at[step],
            recv_sem=recv_sem.at[step],
            device_id={axis: other},
            device_id_type=MESH,
        )
        copy.start()
        copy.wait()
        total = table[pl.ds(keep, size), :] + landing[step][...]
        if step < count - 1:
            table[pl.ds(keep, size), :] = total
        else:
            out_ref[pl.ds(keep, size), :] = total
        base = keep
        bases.append(keep)
    for step in reversed(range(count)):
        axis, other, high = partners[step]
        held = pl.multiple_of(bases[step], 16)
        copy = pltpu.make_async_remote_copy(
            src_ref=out_ref.at[pl.ds(held, size)],
            dst_ref=out_ref.at[pl.ds(held, size)],
            send_sem=send_sem.at[count + step],
            recv_sem=recv_sem.at[count + step],
            device_id={axis: other},
            device_id_type=MESH,
        )
        copy.start()
        copy.wait()
        size *= 2


def gather_picks(library, local_all):
    picks = local_all.shape[0]
    features = library.shape[1]
    sizes = {axis: lax.axis_size(axis) for axis in SPREAD}
    stages = exchange_stages(sizes)
    scratch = [pltpu.VMEM((picks, features), jnp.bfloat16)]
    size = picks
    for _ in stages:
        size //= 2
        scratch.append(pltpu.VMEM((size, features), jnp.bfloat16))
    scratch += [pltpu.SemaphoreType.DMA((2 * len(stages),))] * 2
    return pl.pallas_call(
        functools.partial(gather_kernel, stages),
        out_shape=jax.ShapeDtypeStruct((picks, features), jnp.bfloat16),
        in_specs=[pl.BlockSpec(memory_space=pltpu.VMEM)] * 2,
        out_specs=pl.BlockSpec(memory_space=pltpu.VMEM),
        scratch_shapes=scratch,
        compiler_params=pltpu.CompilerParams(
            collective_id=0, has_side_effects=True, vmem_limit_bytes=40 * 2**20
        ),
        name="gather_picks",
    )(local_all[:, None], library)


def eliminate(left, right):
    size = left.shape[0]
    sub = lax.broadcasted_iota(jnp.int32, (GROUP, size), 0)
    for start in range(0, size, GROUP):
        stop = start + GROUP
        top = left[start:stop, :]
        low = right[start:stop, :]
        columns = [
            jnp.broadcast_to(top[:, start + j : start + j + 1], (GROUP, size)) for j in range(GROUP)
        ]
        pivots = jnp.ones((GROUP, size), jnp.float32)
        for j in range(GROUP):
            pivot = columns[j][j : j + 1, :]
            pivots = jnp.where(sub == j, pivot, pivots)
            factor = jnp.where(sub > j, columns[j] * (1.0 / pivot), 0.0)
            top = top - factor * top[j : j + 1, :]
            low = low - factor * low[j : j + 1, :]
            for k in range(j + 1, GROUP):
                columns[k] = columns[k] - factor * columns[k][j : j + 1, :]
        scale = lax.rsqrt(pivots)
        top = top * scale
        low = low * scale
        right[start:stop, :] = low
        if stop < size:
            side = jnp.transpose(top)[stop:, :]
            both = jnp.concatenate([top, low], axis=1)
            update = jnp.dot(side, both, precision=HIGHEST, preferred_element_type=jnp.float32)
            left[stop:, :] = left[stop:, :] - update[:, :size]
            right[stop:, :] = right[stop:, :] - update[:, size:]


def identity_of(size):
    ones = lax.broadcasted_iota(jnp.int32, (size, size), 0) == lax.broadcasted_iota(
        jnp.int32, (size, size), 1
    )
    return ones.astype(jnp.float32)


def inverse_kernel(first_ref, cross_ref, second_ref, inverse_ref, prior_ref, left):
    size = first_ref.shape[0]
    eye = identity_of(size)
    left[...] = first_ref[...]
    inverse_ref[0] = eye
    eliminate(left, inverse_ref.at[0])
    prior = jnp.dot(
        inverse_ref[0], cross_ref[...], precision=HIGHEST, preferred_element_type=jnp.float32
    )
    prior_t = jnp.transpose(prior)
    prior_ref[...] = prior_t
    left[...] = second_ref[...] - jnp.dot(
        prior_t, prior, precision=HIGHEST, preferred_element_type=jnp.float32
    )
    inverse_ref[1] = eye
    eliminate(left, inverse_ref.at[1])


def inverses(first, cross, second):
    size = first.shape[0]
    vmem = pl.BlockSpec(memory_space=pltpu.VMEM)
    return pl.pallas_call(
        inverse_kernel,
        out_shape=(
            jax.ShapeDtypeStruct((2, size, size), jnp.float32),
            jax.ShapeDtypeStruct((size, size), jnp.float32),
        ),
        in_specs=[vmem] * 3,
        out_specs=(vmem, vmem),
        scratch_shapes=[pltpu.VMEM((size, size), jnp.float32)],
        compiler_params=pltpu.CompilerParams(vmem_limit_bytes=24 * 2**20),
        name="inverses",
    )(first, cross, second)


def local(library, pick_order):
    local_rows = library.shape[0]
    devices = lax.axis_size(SPREAD)
    owned_count = BLOCK // devices
    first_row = lax.axis_index(SPREAD) * local_rows
    row_ids = first_row + jnp.arange(local_rows, dtype=jnp.int32)
    local_all = pick_order - first_row
    if pick_order.shape[0] % (16 * devices) == 0:
        pick_rows = gather_picks(library, local_all)
    else:
        owned_all = ((local_all >= 0) & (local_all < local_rows)).astype(jnp.float32)
        pick_rows = lax.psum(pick_table(library, local_all, owned_all), SPREAD)
        pick_rows = pick_rows.astype(jnp.bfloat16)
    squares = jnp.sum(jnp.square(library.astype(jnp.float32)), axis=1)
    pick_squares = jnp.sum(jnp.square(pick_rows.astype(jnp.float32)), axis=1)
    pick_products = jnp.dot(pick_rows, pick_rows.T, preferred_element_type=jnp.float32)
    pivot = tanimoto(pick_products, pick_squares, pick_squares)
    pivot = pivot + nugget * jnp.eye(pivot.shape[0], dtype=jnp.float32)
    inverse, prior_rows = inverses(
        pivot[:BLOCK, :BLOCK], pivot[:BLOCK, BLOCK:], pivot[BLOCK:, BLOCK:]
    )
    products = jnp.einsum("sf,nf->sn", pick_rows, library, preferred_element_type=jnp.float32)
    marker = (pick_order[:, None] == row_ids[None, :]).astype(jnp.float32)
    kernel = tanimoto(products, pick_squares, squares) + nugget * marker
    first = jnp.dot(inverse[0], kernel[:BLOCK], precision=HIGHEST)
    moved = regroup(first.astype(jnp.bfloat16))
    residual = kernel[BLOCK:] - jnp.dot(prior_rows, first, precision=HIGHEST)
    second = jnp.dot(inverse[1], residual, precision=HIGHEST)
    results = [center_rows(moved, owned_count)]
    results.append(center_rows(regroup(second.astype(jnp.bfloat16)), owned_count))
    return jnp.stack(results, axis=0)


def solution(mesh):
    placed = (P(("groups", "rows", "cols", "sub"), None), P("groups"))
    return jax.shard_map(
        local,
        mesh=mesh,
        in_specs=placed,
        out_specs=P("groups", ("rows", "cols", "sub"), None),
        check_vma=False,
    )
```

```python
import functools

import jax
import jax.numpy as jnp
from jax import lax
from jax.experimental import pallas as pl
from jax.experimental.pallas import tpu as pltpu
from jax.sharding import PartitionSpec as P

BLOCK = 128
BLOCKS = 2
GROUP = 16
SPREAD = ("rows", "cols", "sub")
MESH = pl.DeviceIdType.MESH
HIGHEST = lax.Precision.HIGHEST

nugget = 0.1


def tanimoto(products, left_sq, right_sq):
    return products / (left_sq[:, None] + right_sq[None, :] - products)


def pick_table(library, local_picks, owned_mask):
    clipped = jnp.clip(local_picks, 0, library.shape[0] - 1)
    taken = jnp.take(library, clipped, axis=0).astype(jnp.float32)
    return taken * owned_mask[:, None]


def regroup(block_panel):
    block_count, local_rows = block_panel.shape
    devices_all = lax.axis_size(SPREAD)
    shaped = block_panel.reshape(devices_all, block_count // devices_all, 1, local_rows)
    moved = lax.all_to_all(shaped, SPREAD, split_axis=0, concat_axis=2, tiled=True)
    return moved


def center_rows(moved, owned_count):
    values = moved.reshape(owned_count, -1).astype(jnp.float32)
    column_mean = jnp.mean(values, axis=1, keepdims=True)
    return (values - column_mean).astype(jnp.bfloat16)


def tile_kernel(products, left_sq, right_sq):
    return products / (left_sq + right_sq - products)


def transposed_dot(left, right):
    return lax.dot_general(
        left, right, (((1,), (1,)), ((), ())), preferred_element_type=jnp.float32
    )


def gather_kernel(local_ref, library_ref, kernel_ref, pivot_ref, table, picked, near, far, squares, sub_sem, far_sem):
    sub = lax.axis_index("sub")
    row, col = lax.axis_index("rows"), lax.axis_index("cols")
    row_count, col_count = lax.axis_size("rows"), lax.axis_size("cols")
    chips = row_count * col_count
    me = row * col_count + col
    picks, features = table.shape
    rows = library_ref.shape[0]
    half = BLOCK // 2
    part_rows, part_cols = half // row_count, features // col_count
    other = 1 - sub

    def place(index):
        return {"rows": index // col_count, "cols": lax.rem(index, col_count)}

    barrier = pltpu.get_barrier_semaphore()
    pl.semaphore_signal(barrier, inc=1, device_id={"sub": other}, device_id_type=MESH)
    for k in range(1, chips):
        pl.semaphore_signal(
            barrier, inc=1, device_id=place(lax.rem(me + k, chips)), device_id_type=MESH
        )

    def half_rows(block, which):
        return pl.ds(pl.multiple_of(block * BLOCK + which * half, 16), half)

    def part(ref, block, index):
        first = block * BLOCK + sub * half + (index // col_count) * part_rows
        side = lax.rem(index, col_count) * part_cols
        return ref.at[
            pl.ds(pl.multiple_of(first, 16), part_rows),
            pl.ds(pl.multiple_of(side, 128), part_cols),
        ]

    def sub_copy(source, target, slot):
        return pltpu.make_async_remote_copy(
            src_ref=source,
            dst_ref=target,
            send_sem=sub_sem.at[0, slot],
            recv_sem=sub_sem.at[1, slot],
            device_id={"sub": other},
            device_id_type=MESH,
        )

    def far_copy(source, target, slot, k):
        return pltpu.make_async_remote_copy(
            src_ref=source,
            dst_ref=target,
            send_sem=far_sem.at[0, slot, k - 1],
            recv_sem=far_sem.at[1, slot, k - 1],
            device_id=place(lax.rem(me + k, chips)),
            device_id_type=MESH,
        )

    order = sorted(range(1, chips), key=lambda k: -min(k, chips - k))
    tile = 256
    first = []
    for block in range(BLOCKS):
        span = pl.ds(block * BLOCK, BLOCK)
        hot = local_ref[span, :] == lax.broadcasted_iota(jnp.int32, (BLOCK, rows), 1)
        hot = hot.astype(jnp.float32).astype(jnp.bfloat16)
        for start in range(0, features, tile):
            table[span, start : start + tile] = jnp.dot(
                hot, library_ref[:, start : start + tile], preferred_element_type=jnp.float32
            ).astype(jnp.bfloat16)
        if block == 0:
            pl.semaphore_wait(barrier, chips)
        copy = sub_copy(table.at[half_rows(block, other)], near.at[block], block)
        copy.start()
        first.append(copy)
    second = []
    for block in range(BLOCKS):
        first[block].wait()
        keep = half_rows(block, sub)
        table[keep, :] = table[keep, :] + near[block]
        copies = []
        for k in order:
            copy = far_copy(
                part(table, block, lax.rem(me + k, chips)), far.at[block, k - 1], block, k
            )
            copy.start()
            copies.append(copy)
        second.append(copies)
    ones = jnp.ones((8, features), jnp.bfloat16)
    for start in range(0, rows, tile):
        values = library_ref[start : start + tile, :].astype(jnp.float32)
        values = values * values
        high = values.astype(jnp.bfloat16)
        low = (values - high.astype(jnp.float32)).astype(jnp.bfloat16)
        squares[:, start : start + tile] = transposed_dot(ones, high) + transposed_dot(ones, low)
    third = []
    for block in range(BLOCKS):
        for copy in second[block]:
            copy.wait()
        total = part(table, block, me)[...]
        for k in range(1, chips):
            total = total + far[block, k - 1]
        mine = part(picked, block, me)
        mine[...] = total
        copies = []
        for k in order:
            copy = far_copy(mine, mine, BLOCKS + block, k)
            copy.start()
            copies.append(copy)
        third.append(copies)
    fourth = []
    for block in range(BLOCKS):
        for copy in third[block]:
            copy.wait()
        held = picked.at[half_rows(block, sub)]
        copy = sub_copy(held, held, BLOCKS + block)
        copy.start()
        fourth.append(copy)
    for copy in fourth:
        copy.wait()

    rows_all = picked[...]
    grams = transposed_dot(rows_all, rows_all)
    eye = identity_of(picks)
    across = jnp.sum(grams * eye, axis=0, keepdims=True)
    down = jnp.sum(grams * eye, axis=1, keepdims=True)
    pivot_ref[...] = tile_kernel(grams, down, across) + nugget * eye
    for start in range(0, rows, tile):
        span = slice(start, start + tile)
        products = transposed_dot(rows_all, library_ref[span, :])
        ids = start + lax.broadcasted_iota(jnp.int32, (picks, tile), 1)
        marker = (local_ref[...] == ids).astype(jnp.float32)
        kernel_ref[:, span] = (
            tile_kernel(products, down, squares[0:1, span]) + nugget * marker
        )


def gather_kernels(library, local_all):
    picks = local_all.shape[0]
    rows, features = library.shape
    row_count, col_count = lax.axis_size("rows"), lax.axis_size("cols")
    chips = row_count * col_count
    vmem = pl.BlockSpec(memory_space=pltpu.VMEM)
    half = BLOCK // 2
    return pl.pallas_call(
        gather_kernel,
        out_shape=(
            jax.ShapeDtypeStruct((picks, rows), jnp.float32),
            jax.ShapeDtypeStruct((picks, picks), jnp.float32),
        ),
        in_specs=[vmem] * 2,
        out_specs=(vmem, vmem),
        scratch_shapes=[
            pltpu.VMEM((picks, features), jnp.bfloat16),
            pltpu.VMEM((picks, features), jnp.bfloat16),
            pltpu.VMEM((BLOCKS, half, features), jnp.bfloat16),
            pltpu.VMEM(
                (BLOCKS, chips - 1, half // row_count, features // col_count), jnp.bfloat16
            ),
            pltpu.VMEM((8, rows), jnp.float32),
            pltpu.SemaphoreType.DMA((2, 2 * BLOCKS)),
            pltpu.SemaphoreType.DMA((2, 2 * BLOCKS, chips - 1)),
        ],
        compiler_params=pltpu.CompilerParams(
            collective_id=0, has_side_effects=True, vmem_limit_bytes=40 * 2**20
        ),
        name="gather_kernels",
    )(local_all[:, None], library)


def eliminate(left, right):
    size = left.shape[0]
    sub = lax.broadcasted_iota(jnp.int32, (GROUP, size), 0)
    for start in range(0, size, GROUP):
        stop = start + GROUP
        top = left[start:stop, :]
        low = right[start:stop, :]
        columns = [
            jnp.broadcast_to(top[:, start + j : start + j + 1], (GROUP, size)) for j in range(GROUP)
        ]
        pivots = jnp.ones((GROUP, size), jnp.float32)
        for j in range(GROUP):
            pivot = columns[j][j : j + 1, :]
            pivots = jnp.where(sub == j, pivot, pivots)
            factor = jnp.where(sub > j, columns[j] * (1.0 / pivot), 0.0)
            top = top - factor * top[j : j + 1, :]
            low = low - factor * low[j : j + 1, :]
            for k in range(j + 1, GROUP):
                columns[k] = columns[k] - factor * columns[k][j : j + 1, :]
        scale = lax.rsqrt(pivots)
        top = top * scale
        low = low * scale
        right[start:stop, :] = low
        if stop < size:
            side = jnp.transpose(top)[stop:, :]
            both = jnp.concatenate([top, low], axis=1)
            update = jnp.dot(side, both, precision=HIGHEST, preferred_element_type=jnp.float32)
            left[stop:, :] = left[stop:, :] - update[:, :size]
            right[stop:, :] = right[stop:, :] - update[:, size:]


def identity_of(size):
    ones = lax.broadcasted_iota(jnp.int32, (size, size), 0) == lax.broadcasted_iota(
        jnp.int32, (size, size), 1
    )
    return ones.astype(jnp.float32)


def full_dot(left, right):
    return jnp.dot(left, right, precision=HIGHEST, preferred_element_type=jnp.float32)


def first_kernel(pivot_ref, inverse_ref, prior_ref, second_ref, left):
    left[...] = pivot_ref[:BLOCK, :BLOCK]
    inverse_ref[...] = identity_of(BLOCK)
    eliminate(left, inverse_ref)
    prior = full_dot(inverse_ref[...], pivot_ref[:BLOCK, BLOCK:])
    prior_t = jnp.transpose(prior)
    prior_ref[...] = prior_t
    second_ref[...] = pivot_ref[BLOCK:, BLOCK:] - full_dot(prior_t, prior)


def first_inverse(pivot):
    vmem = pl.BlockSpec(memory_space=pltpu.VMEM)
    square = jax.ShapeDtypeStruct((BLOCK, BLOCK), jnp.float32)
    return pl.pallas_call(
        first_kernel,
        out_shape=(square,) * 3,
        in_specs=[vmem],
        out_specs=(vmem,) * 3,
        scratch_shapes=[pltpu.VMEM((BLOCK, BLOCK), jnp.float32)],
        compiler_params=pltpu.CompilerParams(vmem_limit_bytes=24 * 2**20),
        name="first_inverse",
    )(pivot)


def panel_kernel(inverse_ref, prior_ref, second_ref, kernel_ref, out_ref, left, right, panel, sent, landed, send_sem, recv_sem):
    sizes = [lax.axis_size(axis) for axis in SPREAD]
    row_count, col_count, sub_count = sizes
    devices = row_count * col_count * sub_count
    me = lax.axis_index(SPREAD)
    rows = kernel_ref.shape[1]
    owned = BLOCK // devices

    def place(index):
        return {
            "rows": index // (col_count * sub_count),
            "cols": lax.rem(index // sub_count, col_count),
            "sub": lax.rem(index, sub_count),
        }

    barrier = pltpu.get_barrier_semaphore()
    for k in range(1, devices):
        pl.semaphore_signal(
            barrier, inc=1, device_id=place(lax.rem(me + k, devices)), device_id_type=MESH
        )
    tile = 512
    order = sorted(range(1, devices), key=lambda k: -min(k, devices - k))
    copies = []
    for block in range(BLOCKS):
        if block > 0:
            left[...] = second_ref[...]
            right[...] = identity_of(BLOCK)
            eliminate(left, right)
        for start in range(0, rows, tile):
            span = slice(start, start + tile)
            if block == 0:
                values = full_dot(inverse_ref[...], kernel_ref[:BLOCK, span])
                panel[:, span] = values
            else:
                residual = kernel_ref[BLOCK:, span] - full_dot(prior_ref[...], panel[:, span])
                values = full_dot(right[...], residual)
            sent[block, :, :, span] = values.reshape(devices, owned, tile).astype(jnp.bfloat16)
        if block == 0:
            pl.semaphore_wait(barrier, devices - 1)
        started = []
        for k in order:
            peer = lax.rem(me + k, devices)
            copy = pltpu.make_async_remote_copy(
                src_ref=sent.at[block, peer],
                dst_ref=landed.at[block, k - 1],
                send_sem=send_sem.at[block, k - 1],
                recv_sem=recv_sem.at[block, k - 1],
                device_id=place(peer),
                device_id_type=MESH,
            )
            copy.start()
            started.append(copy)
        copies.append(started)
    for block in range(BLOCKS):
        own = sent[block, me].astype(jnp.float32)
        total = jnp.sum(own, axis=1, keepdims=True)
        for k, copy in zip(order, copies[block]):
            copy.wait()
            total = total + jnp.sum(
                landed[block, k - 1].astype(jnp.float32), axis=1, keepdims=True
            )
        mean = total / (devices * rows)
        for k in range(devices):
            values = sent[block, me] if k == 0 else landed[block, k - 1]
            source = lax.rem(me + devices - k, devices)
            span = pl.ds(pl.multiple_of(source * rows, 128), rows)
            out_ref[block, :, span] = (values.astype(jnp.float32) - mean).astype(jnp.bfloat16)


def centered_panels(inverse, prior_rows, second, kernel):
    rows = kernel.shape[1]
    devices = lax.axis_size(SPREAD)
    owned = BLOCK // devices
    vmem = pl.BlockSpec(memory_space=pltpu.VMEM)
    return pl.pallas_call(
        panel_kernel,
        out_shape=jax.ShapeDtypeStruct((BLOCKS, owned, devices * rows), jnp.bfloat16),
        in_specs=[vmem] * 4,
        out_specs=vmem,
        scratch_shapes=[
            pltpu.VMEM((BLOCK, BLOCK), jnp.float32),
            pltpu.VMEM((BLOCK, BLOCK), jnp.float32),
            pltpu.VMEM((BLOCK, rows), jnp.float32),
            pltpu.VMEM((BLOCKS, devices, owned, rows), jnp.bfloat16),
            pltpu.VMEM((BLOCKS, devices - 1, owned, rows), jnp.bfloat16),
            pltpu.SemaphoreType.DMA((BLOCKS, devices - 1)),
            pltpu.SemaphoreType.DMA((BLOCKS, devices - 1)),
        ],
        compiler_params=pltpu.CompilerParams(
            collective_id=1, has_side_effects=True, vmem_limit_bytes=40 * 2**20
        ),
        name="centered_panels",
    )(inverse, prior_rows, second, kernel)


def whole(pick_rows, library, pick_order, row_ids):
    squares = jnp.sum(jnp.square(library.astype(jnp.float32)), axis=1)
    pick_squares = jnp.sum(jnp.square(pick_rows.astype(jnp.float32)), axis=1)
    pick_products = jnp.dot(pick_rows, pick_rows.T, preferred_element_type=jnp.float32)
    pivot = tanimoto(pick_products, pick_squares, pick_squares)
    pivot = pivot + nugget * jnp.eye(pivot.shape[0], dtype=jnp.float32)
    products = jnp.einsum("sf,nf->sn", pick_rows, library, preferred_element_type=jnp.float32)
    marker = (pick_order[:, None] == row_ids[None, :]).astype(jnp.float32)
    return tanimoto(products, pick_squares, squares) + nugget * marker, pivot


def local(library, pick_order):
    local_rows, features = library.shape
    sizes = {axis: lax.axis_size(axis) for axis in SPREAD}
    devices = lax.axis_size(SPREAD)
    owned_count = BLOCK // devices
    first_row = lax.axis_index(SPREAD) * local_rows
    local_all = pick_order - first_row
    fits = (
        sizes["sub"] == 2
        and BLOCK % (2 * sizes["rows"] * 16) == 0
        and features % (sizes["cols"] * 128) == 0
        and BLOCK % (devices * 8) == 0
        and local_rows % 512 == 0
        and features % 256 == 0
    )
    if fits:
        kernel, pivot = gather_kernels(library, local_all)
        inverse, prior_rows, second = first_inverse(pivot)
        return centered_panels(inverse, prior_rows, second, kernel)
    owned_all = ((local_all >= 0) & (local_all < local_rows)).astype(jnp.float32)
    pick_rows = lax.psum(pick_table(library, local_all, owned_all), SPREAD)
    row_ids = first_row + jnp.arange(local_rows, dtype=jnp.int32)
    kernel, pivot = whole(pick_rows.astype(jnp.bfloat16), library, pick_order, row_ids)
    inverse, prior_rows, second = first_inverse(pivot)
    panel = jnp.dot(inverse, kernel[:BLOCK], precision=HIGHEST)
    moved = regroup(panel.astype(jnp.bfloat16))
    lower = jnp.linalg.cholesky(second)
    identity = jnp.eye(BLOCK, dtype=jnp.float32)
    inverse = lax.linalg.triangular_solve(lower, identity, left_side=True, lower=True)
    residual = kernel[BLOCK:] - jnp.dot(prior_rows, panel, precision=HIGHEST)
    panel = jnp.dot(inverse, residual, precision=HIGHEST)
    results = [center_rows(moved, owned_count)]
    results.append(center_rows(regroup(panel.astype(jnp.bfloat16)), owned_count))
    return jnp.stack(results, axis=0)


def solution(mesh):
    placed = (P(("groups", "rows", "cols", "sub"), None), P("groups"))
    return jax.shard_map(
        local,
        mesh=mesh,
        in_specs=placed,
        out_specs=P("groups", ("rows", "cols", "sub"), None),
        check_vma=False,
    )
```

```python
import functools

import jax
import jax.numpy as jnp
from jax import lax
from jax.experimental import pallas as pl
from jax.experimental.pallas import tpu as pltpu
from jax.sharding import PartitionSpec as P

BLOCK = 128
BLOCKS = 2
GROUP = 16
SPREAD = ("rows", "cols", "sub")
MESH = pl.DeviceIdType.MESH
HIGHEST = lax.Precision.HIGHEST

nugget = 0.1


def tanimoto(products, left_sq, right_sq):
    return products / (left_sq[:, None] + right_sq[None, :] - products)


def pick_table(library, local_picks, owned_mask):
    clipped = jnp.clip(local_picks, 0, library.shape[0] - 1)
    taken = jnp.take(library, clipped, axis=0).astype(jnp.float32)
    return taken * owned_mask[:, None]


def regroup(block_panel):
    block_count, local_rows = block_panel.shape
    devices_all = lax.axis_size(SPREAD)
    shaped = block_panel.reshape(devices_all, block_count // devices_all, 1, local_rows)
    moved = lax.all_to_all(shaped, SPREAD, split_axis=0, concat_axis=2, tiled=True)
    return moved


def center_rows(moved, owned_count):
    values = moved.reshape(owned_count, -1).astype(jnp.float32)
    column_mean = jnp.mean(values, axis=1, keepdims=True)
    return (values - column_mean).astype(jnp.bfloat16)


def eliminate(left, right, hooks=None):
    size = left.shape[0]
    sub = lax.broadcasted_iota(jnp.int32, (GROUP, size), 0)
    for start in range(0, size, GROUP):
        stop = start + GROUP
        top = left[start:stop, :]
        low = right[start:stop, :]
        columns = [
            jnp.broadcast_to(top[:, start + j : start + j + 1], (GROUP, size)) for j in range(GROUP)
        ]
        pivots = jnp.ones((GROUP, size), jnp.float32)
        for j in range(GROUP):
            pivot = columns[j][j : j + 1, :]
            pivots = jnp.where(sub == j, pivot, pivots)
            factor = jnp.where(sub > j, columns[j] * (1.0 / pivot), 0.0)
            top = top - factor * top[j : j + 1, :]
            low = low - factor * low[j : j + 1, :]
            for k in range(j + 1, GROUP):
                columns[k] = columns[k] - factor * columns[k][j : j + 1, :]
        scale = lax.rsqrt(pivots)
        top = top * scale
        low = low * scale
        right[start:stop, :] = low
        if stop < size:
            side = jnp.transpose(top)[stop:, :]
            both = jnp.concatenate([top, low], axis=1)
            update = jnp.dot(side, both, precision=HIGHEST, preferred_element_type=jnp.float32)
            left[stop:, :] = left[stop:, :] - update[:, :size]
            right[stop:, :] = right[stop:, :] - update[:, size:]
        if hooks and start in hooks:
            hooks[start]()


def identity_of(size):
    ones = lax.broadcasted_iota(jnp.int32, (size, size), 0) == lax.broadcasted_iota(
        jnp.int32, (size, size), 1
    )
    return ones.astype(jnp.float32)


def full_dot(left, right):
    return jnp.dot(left, right, precision=HIGHEST, preferred_element_type=jnp.float32)


def first_kernel(pivot_ref, inverse_ref, prior_ref, second_ref, left):
    left[...] = pivot_ref[:BLOCK, :BLOCK]
    inverse_ref[...] = identity_of(BLOCK)
    eliminate(left, inverse_ref)
    prior = full_dot(inverse_ref[...], pivot_ref[:BLOCK, BLOCK:])
    prior_t = jnp.transpose(prior)
    prior_ref[...] = prior_t
    second_ref[...] = pivot_ref[BLOCK:, BLOCK:] - full_dot(prior_t, prior)


def first_inverse(pivot):
    vmem = pl.BlockSpec(memory_space=pltpu.VMEM)
    square = jax.ShapeDtypeStruct((BLOCK, BLOCK), jnp.float32)
    return pl.pallas_call(
        first_kernel,
        out_shape=(square,) * 3,
        in_specs=[vmem],
        out_specs=(vmem,) * 3,
        scratch_shapes=[pltpu.VMEM((BLOCK, BLOCK), jnp.float32)],
        compiler_params=pltpu.CompilerParams(vmem_limit_bytes=24 * 2**20),
        name="first_inverse",
    )(pivot)


def tile_kernel(products, left_sq, right_sq):
    return products / (left_sq + right_sq - products)


def transposed_dot(left, right):
    return lax.dot_general(
        left, right, (((1,), (1,)), ((), ())), preferred_element_type=jnp.float32
    )


def fused_kernel(
    local_ref, library_ref, out_ref,
    table, picked, near, far, squares, kernel, left, right, panel, sent, landed,
    sub_sem, far_sem, send_sem, recv_sem,
):
    sub = lax.axis_index("sub")
    row, col = lax.axis_index("rows"), lax.axis_index("cols")
    row_count, col_count = lax.axis_size("rows"), lax.axis_size("cols")
    chips = row_count * col_count
    devices = 2 * chips
    chip = row * col_count + col
    me = chip * 2 + sub
    features = table.shape[1]
    rows = library_ref.shape[0]
    half = BLOCK // 2
    owned = BLOCK // devices
    part_rows, part_cols = half // row_count, features // col_count
    other = 1 - sub

    def chip_of(index):
        return {"rows": index // col_count, "cols": lax.rem(index, col_count)}

    def device_of(index):
        return {**chip_of(index // 2), "sub": lax.rem(index, 2)}

    barrier = pltpu.get_barrier_semaphore()
    for k in range(1, devices):
        pl.semaphore_signal(
            barrier, inc=1, device_id=device_of(lax.rem(me + k, devices)), device_id_type=MESH
        )

    def half_rows(block, which):
        return pl.ds(pl.multiple_of(block * BLOCK + which * half, 16), half)

    def part(ref, block, index):
        first = block * BLOCK + sub * half + (index // col_count) * part_rows
        side = lax.rem(index, col_count) * part_cols
        return ref.at[
            pl.ds(pl.multiple_of(first, 16), part_rows),
            pl.ds(pl.multiple_of(side, 128), part_cols),
        ]

    def sub_copy(source, target, slot):
        copy = pltpu.make_async_remote_copy(
            src_ref=source,
            dst_ref=target,
            send_sem=sub_sem.at[0, slot],
            recv_sem=sub_sem.at[1, slot],
            device_id={"sub": other},
            device_id_type=MESH,
        )
        copy.start()
        return copy

    def far_copy(source, target, slot, k):
        copy = pltpu.make_async_remote_copy(
            src_ref=source,
            dst_ref=target,
            send_sem=far_sem.at[0, slot, k - 1],
            recv_sem=far_sem.at[1, slot, k - 1],
            device_id=chip_of(lax.rem(chip + k, chips)),
            device_id_type=MESH,
        )
        copy.start()
        return copy

    chip_order = sorted(range(1, chips), key=lambda k: -min(k, chips - k))
    device_order = sorted(range(1, devices), key=lambda k: -min(k, devices - k))
    flights = {}
    tile = 256

    def block_rows(block):
        return slice(block * BLOCK, (block + 1) * BLOCK)

    def pick_block(block):
        span = block_rows(block)
        hot = local_ref[span, :] == lax.broadcasted_iota(jnp.int32, (BLOCK, rows), 1)
        hot = hot.astype(jnp.float32).astype(jnp.bfloat16)
        for start in range(0, features, tile):
            table[span, start : start + tile] = jnp.dot(
                hot, library_ref[:, start : start + tile], preferred_element_type=jnp.float32
            ).astype(jnp.bfloat16)

    def halve(block):
        flights["halve", block] = sub_copy(
            table.at[half_rows(block, other)], near.at[block], block
        )

    def scatter(block):
        flights["halve", block].wait()
        keep = half_rows(block, sub)
        table[keep, :] = table[keep, :] + near[block]
        flights["scatter", block] = [
            far_copy(
                part(table, block, lax.rem(chip + k, chips)), far.at[block, k - 1], block, k
            )
            for k in chip_order
        ]

    def spread(block):
        for copy in flights["scatter", block]:
            copy.wait()
        total = part(table, block, chip)[...]
        for k in range(1, chips):
            total = total + far[block, k - 1]
        mine = part(picked, block, chip)
        mine[...] = total
        flights["spread", block] = [far_copy(mine, mine, BLOCKS + block, k) for k in chip_order]

    def share(block):
        for copy in flights["spread", block]:
            copy.wait()
        held = picked.at[half_rows(block, sub)]
        flights["share", block] = sub_copy(held, held, BLOCKS + block)

    def square_rows():
        ones = jnp.ones((8, features), jnp.bfloat16)
        for start in range(0, rows, tile):
            values = library_ref[start : start + tile, :].astype(jnp.float32)
            values = values * values
            high = values.astype(jnp.bfloat16)
            low = (values - high.astype(jnp.float32)).astype(jnp.bfloat16)
            squares[:, start : start + tile] = transposed_dot(ones, high) + transposed_dot(
                ones, low
            )

    eye = identity_of(BLOCK)

    def fill(block):
        span = block_rows(block)
        picks = picked[span, :]
        gram = transposed_dot(picks, picks)
        across = jnp.sum(gram * eye, axis=0, keepdims=True)
        down = jnp.sum(gram * eye, axis=1, keepdims=True)
        for start in range(0, rows, tile):
            cols = slice(start, start + tile)
            products = transposed_dot(picks, library_ref[cols, :])
            ids = start + lax.broadcasted_iota(jnp.int32, (BLOCK, tile), 1)
            marker = (local_ref[span, :] == ids).astype(jnp.float32)
            kernel[span, cols] = (
                tile_kernel(products, down, squares[0:1, cols]) + nugget * marker
            )
        return tile_kernel(gram, down, across) + nugget * eye, across, down

    def send_block(block):
        started = []
        for k in device_order:
            peer = lax.rem(me + k, devices)
            copy = pltpu.make_async_remote_copy(
                src_ref=sent.at[block, peer],
                dst_ref=landed.at[block, k - 1],
                send_sem=send_sem.at[block, k - 1],
                recv_sem=recv_sem.at[block, k - 1],
                device_id=device_of(peer),
                device_id_type=MESH,
            )
            copy.start()
            started.append(copy)
        flights["send", block] = started

    wide = 512

    def keep_panel(block, span, values):
        sent[block, :, :, span] = values.reshape(devices, owned, wide).astype(jnp.bfloat16)

    def center(block):
        total = jnp.sum(sent[block, me].astype(jnp.float32), axis=1, keepdims=True)
        for k, copy in zip(device_order, flights["send", block]):
            copy.wait()
            total = total + jnp.sum(
                landed[block, k - 1].astype(jnp.float32), axis=1, keepdims=True
            )
        mean = total / (devices * rows)
        for k in range(devices):
            values = sent[block, me] if k == 0 else landed[block, k - 1]
            source = lax.rem(me + devices - k, devices)
            span = pl.ds(pl.multiple_of(source * rows, 128), rows)
            out_ref[block, :, span] = (values.astype(jnp.float32) - mean).astype(jnp.bfloat16)

    pick_block(0)
    pl.semaphore_wait(barrier, devices - 1)
    halve(0)
    pick_block(1)
    halve(1)
    scatter(0)
    square_rows()
    spread(0)
    share(0)
    scatter(1)
    flights["share", 0].wait()
    pivot, across_0, down_0 = fill(0)
    left[...] = pivot
    right[0] = eye
    eliminate(left, right.at[0], {GROUP: lambda: spread(1), 5 * GROUP: lambda: share(1)})
    for start in range(0, rows, wide):
        span = slice(start, start + wide)
        values = full_dot(right[0], kernel[:BLOCK, span])
        panel[:, span] = values
        keep_panel(0, span, values)
    send_block(0)
    flights["share", 1].wait()
    pivot, across_1, down_1 = fill(1)
    cross = transposed_dot(picked[block_rows(0), :], picked[block_rows(1), :])
    prior = full_dot(right[0], tile_kernel(cross, down_0, across_1))
    prior_t = jnp.transpose(prior)
    left[...] = pivot - full_dot(prior_t, prior)
    right[1] = eye
    eliminate(left, right.at[1])
    for start in range(0, rows, wide):
        span = slice(start, start + wide)
        residual = kernel[BLOCK:, span] - full_dot(prior_t, panel[:, span])
        keep_panel(1, span, full_dot(right[1], residual))
    send_block(1)
    for block in range(BLOCKS):
        center(block)


def fused(library, local_all):
    picks = local_all.shape[0]
    rows, features = library.shape
    row_count, col_count = lax.axis_size("rows"), lax.axis_size("cols")
    chips = row_count * col_count
    devices = 2 * chips
    owned = BLOCK // devices
    half = BLOCK // 2
    vmem = pl.BlockSpec(memory_space=pltpu.VMEM)
    return pl.pallas_call(
        fused_kernel,
        out_shape=jax.ShapeDtypeStruct((BLOCKS, owned, devices * rows), jnp.bfloat16),
        in_specs=[vmem] * 2,
        out_specs=vmem,
        scratch_shapes=[
            pltpu.VMEM((picks, features), jnp.bfloat16),
            pltpu.VMEM((picks, features), jnp.bfloat16),
            pltpu.VMEM((BLOCKS, half, features), jnp.bfloat16),
            pltpu.VMEM(
                (BLOCKS, chips - 1, half // row_count, features // col_count), jnp.bfloat16
            ),
            pltpu.VMEM((8, rows), jnp.float32),
            pltpu.VMEM((picks, rows), jnp.float32),
            pltpu.VMEM((BLOCK, BLOCK), jnp.float32),
            pltpu.VMEM((BLOCKS, BLOCK, BLOCK), jnp.float32),
            pltpu.VMEM((BLOCK, rows), jnp.float32),
            pltpu.VMEM((BLOCKS, devices, owned, rows), jnp.bfloat16),
            pltpu.VMEM((BLOCKS, devices - 1, owned, rows), jnp.bfloat16),
            pltpu.SemaphoreType.DMA((2, 2 * BLOCKS)),
            pltpu.SemaphoreType.DMA((2, 2 * BLOCKS, chips - 1)),
            pltpu.SemaphoreType.DMA((BLOCKS, devices - 1)),
            pltpu.SemaphoreType.DMA((BLOCKS, devices - 1)),
        ],
        compiler_params=pltpu.CompilerParams(
            collective_id=0, has_side_effects=True, vmem_limit_bytes=48 * 2**20
        ),
        name="fused",
    )(local_all[:, None], library)


def whole(pick_rows, library, pick_order, row_ids):
    squares = jnp.sum(jnp.square(library.astype(jnp.float32)), axis=1)
    pick_squares = jnp.sum(jnp.square(pick_rows.astype(jnp.float32)), axis=1)
    pick_products = jnp.dot(pick_rows, pick_rows.T, preferred_element_type=jnp.float32)
    pivot = tanimoto(pick_products, pick_squares, pick_squares)
    pivot = pivot + nugget * jnp.eye(pivot.shape[0], dtype=jnp.float32)
    products = jnp.einsum("sf,nf->sn", pick_rows, library, preferred_element_type=jnp.float32)
    marker = (pick_order[:, None] == row_ids[None, :]).astype(jnp.float32)
    return tanimoto(products, pick_squares, squares) + nugget * marker, pivot


def local(library, pick_order):
    local_rows, features = library.shape
    sizes = {axis: lax.axis_size(axis) for axis in SPREAD}
    devices = lax.axis_size(SPREAD)
    owned_count = BLOCK // devices
    first_row = lax.axis_index(SPREAD) * local_rows
    local_all = pick_order - first_row
    fits = (
        sizes["sub"] == 2
        and BLOCK % (2 * sizes["rows"] * 16) == 0
        and features % (sizes["cols"] * 128) == 0
        and BLOCK % (devices * 8) == 0
        and local_rows % 512 == 0
        and features % 256 == 0
    )
    if fits:
        return fused(library, local_all)
    owned_all = ((local_all >= 0) & (local_all < local_rows)).astype(jnp.float32)
    pick_rows = lax.psum(pick_table(library, local_all, owned_all), SPREAD)
    row_ids = first_row + jnp.arange(local_rows, dtype=jnp.int32)
    kernel, pivot = whole(pick_rows.astype(jnp.bfloat16), library, pick_order, row_ids)
    inverse, prior_rows, second = first_inverse(pivot)
    panel = jnp.dot(inverse, kernel[:BLOCK], precision=HIGHEST)
    moved = regroup(panel.astype(jnp.bfloat16))
    lower = jnp.linalg.cholesky(second)
    identity = jnp.eye(BLOCK, dtype=jnp.float32)
    inverse = lax.linalg.triangular_solve(lower, identity, left_side=True, lower=True)
    residual = kernel[BLOCK:] - jnp.dot(prior_rows, panel, precision=HIGHEST)
    panel = jnp.dot(inverse, residual, precision=HIGHEST)
    results = [center_rows(moved, owned_count)]
    results.append(center_rows(regroup(panel.astype(jnp.bfloat16)), owned_count))
    return jnp.stack(results, axis=0)


def solution(mesh):
    placed = (P(("groups", "rows", "cols", "sub"), None), P("groups"))
    return jax.shard_map(
        local,
        mesh=mesh,
        in_specs=placed,
        out_specs=P("groups", ("rows", "cols", "sub"), None),
        check_vma=False,
    )
```

```python
import functools

import jax
import jax.numpy as jnp
from jax import lax
from jax.experimental import pallas as pl
from jax.experimental.pallas import tpu as pltpu
from jax.sharding import PartitionSpec as P

BLOCK = 128
BLOCKS = 2
GROUP = 16
SPREAD = ("rows", "cols", "sub")
MESH = pl.DeviceIdType.MESH
HIGHEST = lax.Precision.HIGHEST

nugget = 0.1


def tanimoto(products, left_sq, right_sq):
    return products / (left_sq[:, None] + right_sq[None, :] - products)


def pick_table(library, local_picks, owned_mask):
    clipped = jnp.clip(local_picks, 0, library.shape[0] - 1)
    taken = jnp.take(library, clipped, axis=0).astype(jnp.float32)
    return taken * owned_mask[:, None]


def regroup(block_panel):
    block_count, local_rows = block_panel.shape
    devices_all = lax.axis_size(SPREAD)
    shaped = block_panel.reshape(devices_all, block_count // devices_all, 1, local_rows)
    moved = lax.all_to_all(shaped, SPREAD, split_axis=0, concat_axis=2, tiled=True)
    return moved


def center_rows(moved, owned_count):
    values = moved.reshape(owned_count, -1).astype(jnp.float32)
    column_mean = jnp.mean(values, axis=1, keepdims=True)
    return (values - column_mean).astype(jnp.bfloat16)


def eliminate(left, right, hooks=None):
    size = left.shape[0]
    sub = lax.broadcasted_iota(jnp.int32, (GROUP, size), 0)
    for start in range(0, size, GROUP):
        stop = start + GROUP
        top = left[start:stop, :]
        low = right[start:stop, :]
        columns = [
            jnp.broadcast_to(top[:, start + j : start + j + 1], (GROUP, size)) for j in range(GROUP)
        ]
        pivots = jnp.ones((GROUP, size), jnp.float32)
        for j in range(GROUP):
            pivot = columns[j][j : j + 1, :]
            pivots = jnp.where(sub == j, pivot, pivots)
            factor = jnp.where(sub > j, columns[j] * (1.0 / pivot), 0.0)
            top = top - factor * top[j : j + 1, :]
            low = low - factor * low[j : j + 1, :]
            for k in range(j + 1, GROUP):
                columns[k] = columns[k] - factor * columns[k][j : j + 1, :]
        scale = lax.rsqrt(pivots)
        top = top * scale
        low = low * scale
        right[start:stop, :] = low
        if stop < size:
            side = jnp.transpose(top)[stop:, :]
            both = jnp.concatenate([top, low], axis=1)
            update = jnp.dot(side, both, precision=HIGHEST, preferred_element_type=jnp.float32)
            left[stop:, :] = left[stop:, :] - update[:, :size]
            right[stop:, :] = right[stop:, :] - update[:, size:]
        if hooks and start in hooks:
            hooks[start]()


def identity_of(size):
    ones = lax.broadcasted_iota(jnp.int32, (size, size), 0) == lax.broadcasted_iota(
        jnp.int32, (size, size), 1
    )
    return ones.astype(jnp.float32)


def full_dot(left, right):
    return jnp.dot(left, right, precision=HIGHEST, preferred_element_type=jnp.float32)


def halves(values):
    high = values.astype(jnp.bfloat16)
    return high, (values - high.astype(jnp.float32)).astype(jnp.bfloat16)


def left_parts(values):
    high, low = halves(values)
    return jnp.concatenate([high, low, high], axis=1)


def split_dot(parts, right):
    high, low = halves(right)
    return jnp.dot(
        parts, jnp.concatenate([high, high, low], axis=0), preferred_element_type=jnp.float32
    )


def first_kernel(pivot_ref, inverse_ref, prior_ref, second_ref, left):
    left[...] = pivot_ref[:BLOCK, :BLOCK]
    inverse_ref[...] = identity_of(BLOCK)
    eliminate(left, inverse_ref)
    prior = full_dot(inverse_ref[...], pivot_ref[:BLOCK, BLOCK:])
    prior_t = jnp.transpose(prior)
    prior_ref[...] = prior_t
    second_ref[...] = pivot_ref[BLOCK:, BLOCK:] - full_dot(prior_t, prior)


def first_inverse(pivot):
    vmem = pl.BlockSpec(memory_space=pltpu.VMEM)
    square = jax.ShapeDtypeStruct((BLOCK, BLOCK), jnp.float32)
    return pl.pallas_call(
        first_kernel,
        out_shape=(square,) * 3,
        in_specs=[vmem],
        out_specs=(vmem,) * 3,
        scratch_shapes=[pltpu.VMEM((BLOCK, BLOCK), jnp.float32)],
        compiler_params=pltpu.CompilerParams(vmem_limit_bytes=24 * 2**20),
        name="first_inverse",
    )(pivot)


def tile_kernel(products, left_sq, right_sq):
    return products / (left_sq + right_sq - products)


def transposed_dot(left, right):
    return lax.dot_general(
        left, right, (((1,), (1,)), ((), ())), preferred_element_type=jnp.float32
    )


def fused_kernel(
    local_ref, library_ref, out_ref,
    table, picked, near, far, squares, kernel, left, right, panel, sent, landed,
    sub_sem, far_sem, send_sem, recv_sem,
):
    sub = lax.axis_index("sub")
    row, col = lax.axis_index("rows"), lax.axis_index("cols")
    row_count, col_count = lax.axis_size("rows"), lax.axis_size("cols")
    chips = row_count * col_count
    devices = 2 * chips
    chip = row * col_count + col
    me = chip * 2 + sub
    features = table.shape[1]
    rows = library_ref.shape[0]
    half = BLOCK // 2
    owned = BLOCK // devices
    part_rows, part_cols = half // row_count, features // col_count
    other = 1 - sub

    def chip_of(index):
        return {"rows": index // col_count, "cols": lax.rem(index, col_count)}

    def device_of(index):
        return {**chip_of(index // 2), "sub": lax.rem(index, 2)}

    barrier = pltpu.get_barrier_semaphore()
    for k in range(1, devices):
        pl.semaphore_signal(
            barrier, inc=1, device_id=device_of(lax.rem(me + k, devices)), device_id_type=MESH
        )

    def half_rows(block, which):
        return pl.ds(pl.multiple_of(block * BLOCK + which * half, 16), half)

    def part(ref, block, index):
        first = block * BLOCK + sub * half + (index // col_count) * part_rows
        side = lax.rem(index, col_count) * part_cols
        return ref.at[
            pl.ds(pl.multiple_of(first, 16), part_rows),
            pl.ds(pl.multiple_of(side, 128), part_cols),
        ]

    def sub_copy(source, target, slot):
        copy = pltpu.make_async_remote_copy(
            src_ref=source,
            dst_ref=target,
            send_sem=sub_sem.at[0, slot],
            recv_sem=sub_sem.at[1, slot],
            device_id={"sub": other},
            device_id_type=MESH,
        )
        copy.start()
        return copy

    def far_copy(source, target, slot, k):
        copy = pltpu.make_async_remote_copy(
            src_ref=source,
            dst_ref=target,
            send_sem=far_sem.at[0, slot, k - 1],
            recv_sem=far_sem.at[1, slot, k - 1],
            device_id=chip_of(lax.rem(chip + k, chips)),
            device_id_type=MESH,
        )
        copy.start()
        return copy

    chip_order = sorted(range(1, chips), key=lambda k: -min(k, chips - k))
    device_order = sorted(range(1, devices), key=lambda k: -min(k, devices - k))
    flights = {}
    tile = 256

    def block_rows(block):
        return slice(block * BLOCK, (block + 1) * BLOCK)

    def pick_block(block):
        span = block_rows(block)
        hot = local_ref[span, :] == lax.broadcasted_iota(jnp.int32, (BLOCK, rows), 1)
        hot = hot.astype(jnp.float32).astype(jnp.bfloat16)
        for start in range(0, features, tile):
            table[span, start : start + tile] = jnp.dot(
                hot, library_ref[:, start : start + tile], preferred_element_type=jnp.float32
            ).astype(jnp.bfloat16)

    def halve(block):
        flights["halve", block] = sub_copy(
            table.at[half_rows(block, other)], near.at[block], block
        )

    def scatter(block):
        flights["halve", block].wait()
        keep = half_rows(block, sub)
        table[keep, :] = table[keep, :] + near[block]
        flights["scatter", block] = [
            far_copy(
                part(table, block, lax.rem(chip + k, chips)), far.at[block, k - 1], block, k
            )
            for k in chip_order
        ]

    def spread(block):
        for copy in flights["scatter", block]:
            copy.wait()
        total = part(table, block, chip)[...]
        for k in range(1, chips):
            total = total + far[block, k - 1]
        mine = part(picked, block, chip)
        mine[...] = total
        flights["spread", block] = [far_copy(mine, mine, BLOCKS + block, k) for k in chip_order]

    def share(block):
        for copy in flights["spread", block]:
            copy.wait()
        held = picked.at[half_rows(block, sub)]
        flights["share", block] = sub_copy(held, held, BLOCKS + block)

    def square_rows():
        for start in range(0, rows, tile):
            values = library_ref[start : start + tile, :].astype(jnp.float32)
            values = values * values
            folded = values[:, :128]
            for first in range(128, features, 128):
                folded = folded + values[:, first : first + 128]
            squares[0:1, start : start + tile] = jnp.sum(
                jnp.transpose(folded), axis=0, keepdims=True
            )

    eye = identity_of(BLOCK)

    def fill(block):
        span = block_rows(block)
        picks = picked[span, :]
        gram = transposed_dot(picks, picks)
        across = jnp.sum(gram * eye, axis=0, keepdims=True)
        down = jnp.sum(gram * eye, axis=1, keepdims=True)
        for start in range(0, rows, tile):
            cols = slice(start, start + tile)
            products = transposed_dot(picks, library_ref[cols, :])
            ids = start + lax.broadcasted_iota(jnp.int32, (BLOCK, tile), 1)
            marker = (local_ref[span, :] == ids).astype(jnp.float32)
            kernel[span, cols] = (
                tile_kernel(products, down, squares[0:1, cols]) + nugget * marker
            )
        return tile_kernel(gram, down, across) + nugget * eye, across, down

    def send_block(block):
        started = []
        for k in device_order:
            peer = lax.rem(me + k, devices)
            copy = pltpu.make_async_remote_copy(
                src_ref=sent.at[block, peer],
                dst_ref=landed.at[block, k - 1],
                send_sem=send_sem.at[block, k - 1],
                recv_sem=recv_sem.at[block, k - 1],
                device_id=device_of(peer),
                device_id_type=MESH,
            )
            copy.start()
            started.append(copy)
        flights["send", block] = started

    wide = 512

    def keep_panel(block, span, values):
        sent[block, :, :, span] = values.reshape(devices, owned, wide).astype(jnp.bfloat16)

    def center(block):
        total = jnp.sum(sent[block, me].astype(jnp.float32), axis=1, keepdims=True)
        for k, copy in zip(device_order, flights["send", block]):
            copy.wait()
            total = total + jnp.sum(
                landed[block, k - 1].astype(jnp.float32), axis=1, keepdims=True
            )
        mean = total / (devices * rows)
        for k in range(devices):
            values = sent[block, me] if k == 0 else landed[block, k - 1]
            source = lax.rem(me + devices - k, devices)
            span = pl.ds(pl.multiple_of(source * rows, 128), rows)
            out_ref[block, :, span] = (values.astype(jnp.float32) - mean).astype(jnp.bfloat16)

    pick_block(0)
    pl.semaphore_wait(barrier, devices - 1)
    halve(0)
    pick_block(1)
    halve(1)
    scatter(0)
    square_rows()
    spread(0)
    share(0)
    scatter(1)
    flights["share", 0].wait()
    pivot, across_0, down_0 = fill(0)
    left[...] = pivot
    right[0] = eye
    eliminate(left, right.at[0], {4 * GROUP: lambda: spread(1)})
    parts = left_parts(right[0])
    for start in range(0, rows, wide):
        span = slice(start, start + wide)
        values = split_dot(parts, kernel[:BLOCK, span])
        panel[:, span] = values
        keep_panel(0, span, values)
    share(1)
    send_block(0)
    flights["share", 1].wait()
    pivot, across_1, down_1 = fill(1)
    cross = transposed_dot(picked[block_rows(0), :], picked[block_rows(1), :])
    prior = full_dot(right[0], tile_kernel(cross, down_0, across_1))
    prior_t = jnp.transpose(prior)
    left[...] = pivot - full_dot(prior_t, prior)
    right[1] = eye
    eliminate(left, right.at[1])
    prior_parts, parts = left_parts(prior_t), left_parts(right[1])
    for start in range(0, rows, wide):
        span = slice(start, start + wide)
        residual = kernel[BLOCK:, span] - split_dot(prior_parts, panel[:, span])
        keep_panel(1, span, split_dot(parts, residual))
    send_block(1)
    for block in range(BLOCKS):
        center(block)


def fused(library, local_all):
    picks = local_all.shape[0]
    rows, features = library.shape
    row_count, col_count = lax.axis_size("rows"), lax.axis_size("cols")
    chips = row_count * col_count
    devices = 2 * chips
    owned = BLOCK // devices
    half = BLOCK // 2
    vmem = pl.BlockSpec(memory_space=pltpu.VMEM)
    return pl.pallas_call(
        fused_kernel,
        out_shape=jax.ShapeDtypeStruct((BLOCKS, owned, devices * rows), jnp.bfloat16),
        in_specs=[vmem] * 2,
        out_specs=vmem,
        scratch_shapes=[
            pltpu.VMEM((picks, features), jnp.bfloat16),
            pltpu.VMEM((picks, features), jnp.bfloat16),
            pltpu.VMEM((BLOCKS, half, features), jnp.bfloat16),
            pltpu.VMEM(
                (BLOCKS, chips - 1, half // row_count, features // col_count), jnp.bfloat16
            ),
            pltpu.VMEM((8, rows), jnp.float32),
            pltpu.VMEM((picks, rows), jnp.float32),
            pltpu.VMEM((BLOCK, BLOCK), jnp.float32),
            pltpu.VMEM((BLOCKS, BLOCK, BLOCK), jnp.float32),
            pltpu.VMEM((BLOCK, rows), jnp.float32),
            pltpu.VMEM((BLOCKS, devices, owned, rows), jnp.bfloat16),
            pltpu.VMEM((BLOCKS, devices - 1, owned, rows), jnp.bfloat16),
            pltpu.SemaphoreType.DMA((2, 2 * BLOCKS)),
            pltpu.SemaphoreType.DMA((2, 2 * BLOCKS, chips - 1)),
            pltpu.SemaphoreType.DMA((BLOCKS, devices - 1)),
            pltpu.SemaphoreType.DMA((BLOCKS, devices - 1)),
        ],
        compiler_params=pltpu.CompilerParams(
            collective_id=0, has_side_effects=True, vmem_limit_bytes=48 * 2**20
        ),
        name="fused",
    )(local_all[:, None], library)


def whole(pick_rows, library, pick_order, row_ids):
    squares = jnp.sum(jnp.square(library.astype(jnp.float32)), axis=1)
    pick_squares = jnp.sum(jnp.square(pick_rows.astype(jnp.float32)), axis=1)
    pick_products = jnp.dot(pick_rows, pick_rows.T, preferred_element_type=jnp.float32)
    pivot = tanimoto(pick_products, pick_squares, pick_squares)
    pivot = pivot + nugget * jnp.eye(pivot.shape[0], dtype=jnp.float32)
    products = jnp.einsum("sf,nf->sn", pick_rows, library, preferred_element_type=jnp.float32)
    marker = (pick_order[:, None] == row_ids[None, :]).astype(jnp.float32)
    return tanimoto(products, pick_squares, squares) + nugget * marker, pivot


def local(library, pick_order):
    local_rows, features = library.shape
    sizes = {axis: lax.axis_size(axis) for axis in SPREAD}
    devices = lax.axis_size(SPREAD)
    owned_count = BLOCK // devices
    first_row = lax.axis_index(SPREAD) * local_rows
    local_all = pick_order - first_row
    fits = (
        sizes["sub"] == 2
        and BLOCK % (2 * sizes["rows"] * 16) == 0
        and features % (sizes["cols"] * 128) == 0
        and BLOCK % (devices * 8) == 0
        and local_rows % 512 == 0
        and features % 256 == 0
    )
    if fits:
        return fused(library, local_all)
    owned_all = ((local_all >= 0) & (local_all < local_rows)).astype(jnp.float32)
    pick_rows = lax.psum(pick_table(library, local_all, owned_all), SPREAD)
    row_ids = first_row + jnp.arange(local_rows, dtype=jnp.int32)
    kernel, pivot = whole(pick_rows.astype(jnp.bfloat16), library, pick_order, row_ids)
    inverse, prior_rows, second = first_inverse(pivot)
    panel = jnp.dot(inverse, kernel[:BLOCK], precision=HIGHEST)
    moved = regroup(panel.astype(jnp.bfloat16))
    lower = jnp.linalg.cholesky(second)
    identity = jnp.eye(BLOCK, dtype=jnp.float32)
    inverse = lax.linalg.triangular_solve(lower, identity, left_side=True, lower=True)
    residual = kernel[BLOCK:] - jnp.dot(prior_rows, panel, precision=HIGHEST)
    panel = jnp.dot(inverse, residual, precision=HIGHEST)
    results = [center_rows(moved, owned_count)]
    results.append(center_rows(regroup(panel.astype(jnp.bfloat16)), owned_count))
    return jnp.stack(results, axis=0)


def solution(mesh):
    placed = (P(("groups", "rows", "cols", "sub"), None), P("groups"))
    return jax.shard_map(
        local,
        mesh=mesh,
        in_specs=placed,
        out_specs=P("groups", ("rows", "cols", "sub"), None),
        check_vma=False,
    )
```

```python
import functools

import jax
import jax.numpy as jnp
from jax import lax
from jax.experimental import pallas as pl
from jax.experimental.pallas import tpu as pltpu
from jax.sharding import PartitionSpec as P

BLOCK = 128
BLOCKS = 2
GROUP = 16
SPREAD = ("rows", "cols", "sub")
MESH = pl.DeviceIdType.MESH
HIGHEST = lax.Precision.HIGHEST

nugget = 0.1


def tanimoto(products, left_sq, right_sq):
    return products / (left_sq[:, None] + right_sq[None, :] - products)


def pick_table(library, local_picks, owned_mask):
    clipped = jnp.clip(local_picks, 0, library.shape[0] - 1)
    taken = jnp.take(library, clipped, axis=0).astype(jnp.float32)
    return taken * owned_mask[:, None]


def regroup(block_panel):
    block_count, local_rows = block_panel.shape
    devices_all = lax.axis_size(SPREAD)
    shaped = block_panel.reshape(devices_all, block_count // devices_all, 1, local_rows)
    moved = lax.all_to_all(shaped, SPREAD, split_axis=0, concat_axis=2, tiled=True)
    return moved


def center_rows(moved, owned_count):
    values = moved.reshape(owned_count, -1).astype(jnp.float32)
    column_mean = jnp.mean(values, axis=1, keepdims=True)
    return (values - column_mean).astype(jnp.bfloat16)


def eliminate(left, right, hooks=None):
    size = left.shape[0]
    sub = lax.broadcasted_iota(jnp.int32, (GROUP, size), 0)
    for start in range(0, size, GROUP):
        stop = start + GROUP
        top = left[start:stop, :]
        low = right[start:stop, :]
        columns = [
            jnp.broadcast_to(top[:, start + j : start + j + 1], (GROUP, size)) for j in range(GROUP)
        ]
        pivots = jnp.ones((GROUP, size), jnp.float32)
        for j in range(GROUP):
            pivot = columns[j][j : j + 1, :]
            pivots = jnp.where(sub == j, pivot, pivots)
            factor = jnp.where(sub > j, columns[j] * (1.0 / pivot), 0.0)
            top = top - factor * top[j : j + 1, :]
            low = low - factor * low[j : j + 1, :]
            for k in range(j + 1, GROUP):
                columns[k] = columns[k] - factor * columns[k][j : j + 1, :]
        scale = lax.rsqrt(pivots)
        top = top * scale
        low = low * scale
        right[start:stop, :] = low
        if stop < size:
            side = jnp.transpose(top)[stop:, :]
            both = jnp.concatenate([top, low], axis=1)
            update = jnp.dot(side, both, precision=HIGHEST, preferred_element_type=jnp.float32)
            left[stop:, :] = left[stop:, :] - update[:, :size]
            right[stop:, :] = right[stop:, :] - update[:, size:]
        if hooks and start in hooks:
            hooks[start]()


def identity_of(size):
    ones = lax.broadcasted_iota(jnp.int32, (size, size), 0) == lax.broadcasted_iota(
        jnp.int32, (size, size), 1
    )
    return ones.astype(jnp.float32)


def full_dot(left, right):
    return jnp.dot(left, right, precision=HIGHEST, preferred_element_type=jnp.float32)


def halves(values):
    high = values.astype(jnp.bfloat16)
    return high, (values - high.astype(jnp.float32)).astype(jnp.bfloat16)


def left_parts(values):
    high, low = halves(values)
    return jnp.concatenate([high, low, high], axis=1)


def split_dot(parts, right):
    high, low = halves(right)
    return jnp.dot(
        parts, jnp.concatenate([high, high, low], axis=0), preferred_element_type=jnp.float32
    )


def first_kernel(pivot_ref, inverse_ref, prior_ref, second_ref, left):
    left[...] = pivot_ref[:BLOCK, :BLOCK]
    inverse_ref[...] = identity_of(BLOCK)
    eliminate(left, inverse_ref)
    prior = full_dot(inverse_ref[...], pivot_ref[:BLOCK, BLOCK:])
    prior_t = jnp.transpose(prior)
    prior_ref[...] = prior_t
    second_ref[...] = pivot_ref[BLOCK:, BLOCK:] - full_dot(prior_t, prior)


def first_inverse(pivot):
    vmem = pl.BlockSpec(memory_space=pltpu.VMEM)
    square = jax.ShapeDtypeStruct((BLOCK, BLOCK), jnp.float32)
    return pl.pallas_call(
        first_kernel,
        out_shape=(square,) * 3,
        in_specs=[vmem],
        out_specs=(vmem,) * 3,
        scratch_shapes=[pltpu.VMEM((BLOCK, BLOCK), jnp.float32)],
        compiler_params=pltpu.CompilerParams(vmem_limit_bytes=24 * 2**20),
        name="first_inverse",
    )(pivot)


def tile_kernel(products, left_sq, right_sq):
    return products / (left_sq + right_sq - products)


def transposed_dot(left, right):
    return lax.dot_general(
        left, right, (((1,), (1,)), ((), ())), preferred_element_type=jnp.float32
    )


def fused_kernel(
    local_ref, library_ref, out_ref,
    table, picked, near, far, squares, kernel, left, right, panel, sent, landed,
    sub_sem, far_sem, send_sem, recv_sem,
):
    sub = lax.axis_index("sub")
    row, col = lax.axis_index("rows"), lax.axis_index("cols")
    row_count, col_count = lax.axis_size("rows"), lax.axis_size("cols")
    chips = row_count * col_count
    devices = 2 * chips
    chip = row * col_count + col
    me = chip * 2 + sub
    features = table.shape[1]
    rows = library_ref.shape[0]
    half = BLOCK // 2
    owned = BLOCK // devices
    part_rows, part_cols = half // row_count, features // col_count
    other = 1 - sub

    def chip_of(index):
        return {"rows": index // col_count, "cols": lax.rem(index, col_count)}

    def device_of(index):
        return {**chip_of(index // 2), "sub": lax.rem(index, 2)}

    barrier = pltpu.get_barrier_semaphore()
    for k in range(1, devices):
        pl.semaphore_signal(
            barrier, inc=1, device_id=device_of(lax.rem(me + k, devices)), device_id_type=MESH
        )

    def half_rows(block, which):
        return pl.ds(pl.multiple_of(block * BLOCK + which * half, 16), half)

    def part(ref, block, index):
        first = block * BLOCK + sub * half + (index // col_count) * part_rows
        side = lax.rem(index, col_count) * part_cols
        return ref.at[
            pl.ds(pl.multiple_of(first, 16), part_rows),
            pl.ds(pl.multiple_of(side, 128), part_cols),
        ]

    def sub_copy(source, target, slot):
        copy = pltpu.make_async_remote_copy(
            src_ref=source,
            dst_ref=target,
            send_sem=sub_sem.at[0, slot],
            recv_sem=sub_sem.at[1, slot],
            device_id={"sub": other},
            device_id_type=MESH,
        )
        copy.start()
        return copy

    def far_copy(source, target, slot, k):
        copy = pltpu.make_async_remote_copy(
            src_ref=source,
            dst_ref=target,
            send_sem=far_sem.at[0, slot, k - 1],
            recv_sem=far_sem.at[1, slot, k - 1],
            device_id=chip_of(lax.rem(chip + k, chips)),
            device_id_type=MESH,
        )
        copy.start()
        return copy

    chip_order = sorted(range(1, chips), key=lambda k: -min(k, chips - k))
    device_order = sorted(range(1, devices), key=lambda k: -min(k, devices - k))
    flights = {}
    tile = 256

    def block_rows(block):
        return slice(block * BLOCK, (block + 1) * BLOCK)

    def pick_block(block):
        span = block_rows(block)
        hot = local_ref[span, :] == lax.broadcasted_iota(jnp.int32, (BLOCK, rows), 1)
        hot = hot.astype(jnp.float32).astype(jnp.bfloat16)
        for start in range(0, features, tile):
            table[span, start : start + tile] = jnp.dot(
                hot, library_ref[:, start : start + tile], preferred_element_type=jnp.float32
            ).astype(jnp.bfloat16)

    def halve(block):
        flights["halve", block] = sub_copy(
            table.at[half_rows(block, other)], near.at[block], block
        )

    def scatter(block):
        flights["halve", block].wait()
        keep = half_rows(block, sub)
        table[keep, :] = table[keep, :] + near[block]
        flights["scatter", block] = [
            far_copy(
                part(table, block, lax.rem(chip + k, chips)), far.at[block, k - 1], block, k
            )
            for k in chip_order
        ]

    def spread(block):
        for copy in flights["scatter", block]:
            copy.wait()
        total = part(table, block, chip)[...]
        for k in range(1, chips):
            total = total + far[block, k - 1]
        mine = part(picked, block, chip)
        mine[...] = total
        flights["spread", block] = [far_copy(mine, mine, BLOCKS + block, k) for k in chip_order]

    def share(block):
        for copy in flights["spread", block]:
            copy.wait()
        held = picked.at[half_rows(block, sub)]
        flights["share", block] = sub_copy(held, held, BLOCKS + block)

    def square_rows():
        for start in range(0, rows, tile):
            values = library_ref[start : start + tile, :].astype(jnp.float32)
            values = values * values
            folded = values[:, :128]
            for first in range(128, features, 128):
                folded = folded + values[:, first : first + 128]
            squares[0:1, start : start + tile] = jnp.sum(
                jnp.transpose(folded), axis=0, keepdims=True
            )

    eye = identity_of(BLOCK)

    def fill(block):
        span = block_rows(block)
        picks = picked[span, :]
        gram = transposed_dot(picks, picks)
        across = jnp.sum(gram * eye, axis=0, keepdims=True)
        down = jnp.sum(gram * eye, axis=1, keepdims=True)
        for start in range(0, rows, tile):
            cols = slice(start, start + tile)
            products = transposed_dot(picks, library_ref[cols, :])
            ids = start + lax.broadcasted_iota(jnp.int32, (BLOCK, tile), 1)
            marker = (local_ref[span, :] == ids).astype(jnp.float32)
            kernel[span, cols] = (
                tile_kernel(products, down, squares[0:1, cols]) + nugget * marker
            )
        return tile_kernel(gram, down, across) + nugget * eye, across, down

    def send_block(block):
        started = []
        for k in device_order:
            peer = lax.rem(me + k, devices)
            copy = pltpu.make_async_remote_copy(
                src_ref=sent.at[block, peer],
                dst_ref=landed.at[block, k - 1],
                send_sem=send_sem.at[block, k - 1],
                recv_sem=recv_sem.at[block, k - 1],
                device_id=device_of(peer),
                device_id_type=MESH,
            )
            copy.start()
            started.append(copy)
        flights["send", block] = started

    wide = 512

    def keep_panel(block, span, values):
        sent[block, :, :, span] = values.reshape(devices, owned, wide).astype(jnp.bfloat16)

    def center(block):
        total = jnp.sum(sent[block, me].astype(jnp.float32), axis=1, keepdims=True)
        for k, copy in zip(device_order, flights["send", block]):
            copy.wait()
            total = total + jnp.sum(
                landed[block, k - 1].astype(jnp.float32), axis=1, keepdims=True
            )
        mean = total / (devices * rows)
        for k in range(devices):
            values = sent[block, me] if k == 0 else landed[block, k - 1]
            source = lax.rem(me + devices - k, devices)
            span = pl.ds(pl.multiple_of(source * rows, 128), rows)
            out_ref[block, :, span] = (values.astype(jnp.float32) - mean).astype(jnp.bfloat16)

    pick_block(0)
    pl.semaphore_wait(barrier, devices - 1)
    halve(0)
    pick_block(1)
    scatter(0)
    halve(1)
    square_rows()
    spread(0)
    share(0)
    scatter(1)
    flights["share", 0].wait()
    pivot, across_0, down_0 = fill(0)
    left[...] = pivot
    right[0] = eye
    eliminate(left, right.at[0], {2 * GROUP: lambda: spread(1)})
    parts = left_parts(right[0])
    for start in range(0, rows, wide):
        span = slice(start, start + wide)
        values = split_dot(parts, kernel[:BLOCK, span])
        panel[:, span] = values
        keep_panel(0, span, values)
    share(1)
    send_block(0)
    flights["share", 1].wait()
    pivot, across_1, down_1 = fill(1)
    cross = transposed_dot(picked[block_rows(0), :], picked[block_rows(1), :])
    prior = full_dot(right[0], tile_kernel(cross, down_0, across_1))
    prior_t = jnp.transpose(prior)
    left[...] = pivot - full_dot(prior_t, prior)
    right[1] = eye
    eliminate(left, right.at[1])
    prior_parts, parts = left_parts(prior_t), left_parts(right[1])
    for start in range(0, rows, wide):
        span = slice(start, start + wide)
        residual = kernel[BLOCK:, span] - split_dot(prior_parts, panel[:, span])
        keep_panel(1, span, split_dot(parts, residual))
    send_block(1)
    for block in range(BLOCKS):
        center(block)


def fused(library, local_all):
    picks = local_all.shape[0]
    rows, features = library.shape
    row_count, col_count = lax.axis_size("rows"), lax.axis_size("cols")
    chips = row_count * col_count
    devices = 2 * chips
    owned = BLOCK // devices
    half = BLOCK // 2
    vmem = pl.BlockSpec(memory_space=pltpu.VMEM)
    return pl.pallas_call(
        fused_kernel,
        out_shape=jax.ShapeDtypeStruct((BLOCKS, owned, devices * rows), jnp.bfloat16),
        in_specs=[vmem] * 2,
        out_specs=vmem,
        scratch_shapes=[
            pltpu.VMEM((picks, features), jnp.bfloat16),
            pltpu.VMEM((picks, features), jnp.bfloat16),
            pltpu.VMEM((BLOCKS, half, features), jnp.bfloat16),
            pltpu.VMEM(
                (BLOCKS, chips - 1, half // row_count, features // col_count), jnp.bfloat16
            ),
            pltpu.VMEM((8, rows), jnp.float32),
            pltpu.VMEM((picks, rows), jnp.float32),
            pltpu.VMEM((BLOCK, BLOCK), jnp.float32),
            pltpu.VMEM((BLOCKS, BLOCK, BLOCK), jnp.float32),
            pltpu.VMEM((BLOCK, rows), jnp.float32),
            pltpu.VMEM((BLOCKS, devices, owned, rows), jnp.bfloat16),
            pltpu.VMEM((BLOCKS, devices - 1, owned, rows), jnp.bfloat16),
            pltpu.SemaphoreType.DMA((2, 2 * BLOCKS)),
            pltpu.SemaphoreType.DMA((2, 2 * BLOCKS, chips - 1)),
            pltpu.SemaphoreType.DMA((BLOCKS, devices - 1)),
            pltpu.SemaphoreType.DMA((BLOCKS, devices - 1)),
        ],
        compiler_params=pltpu.CompilerParams(
            collective_id=0, has_side_effects=True, vmem_limit_bytes=48 * 2**20
        ),
        name="fused",
    )(local_all[:, None], library)


def whole(pick_rows, library, pick_order, row_ids):
    squares = jnp.sum(jnp.square(library.astype(jnp.float32)), axis=1)
    pick_squares = jnp.sum(jnp.square(pick_rows.astype(jnp.float32)), axis=1)
    pick_products = jnp.dot(pick_rows, pick_rows.T, preferred_element_type=jnp.float32)
    pivot = tanimoto(pick_products, pick_squares, pick_squares)
    pivot = pivot + nugget * jnp.eye(pivot.shape[0], dtype=jnp.float32)
    products = jnp.einsum("sf,nf->sn", pick_rows, library, preferred_element_type=jnp.float32)
    marker = (pick_order[:, None] == row_ids[None, :]).astype(jnp.float32)
    return tanimoto(products, pick_squares, squares) + nugget * marker, pivot


def local(library, pick_order):
    local_rows, features = library.shape
    sizes = {axis: lax.axis_size(axis) for axis in SPREAD}
    devices = lax.axis_size(SPREAD)
    owned_count = BLOCK // devices
    first_row = lax.axis_index(SPREAD) * local_rows
    local_all = pick_order - first_row
    fits = (
        sizes["sub"] == 2
        and BLOCK % (2 * sizes["rows"] * 16) == 0
        and features % (sizes["cols"] * 128) == 0
        and BLOCK % (devices * 8) == 0
        and local_rows % 512 == 0
        and features % 256 == 0
    )
    if fits:
        return fused(library, local_all)
    owned_all = ((local_all >= 0) & (local_all < local_rows)).astype(jnp.float32)
    pick_rows = lax.psum(pick_table(library, local_all, owned_all), SPREAD)
    row_ids = first_row + jnp.arange(local_rows, dtype=jnp.int32)
    kernel, pivot = whole(pick_rows.astype(jnp.bfloat16), library, pick_order, row_ids)
    inverse, prior_rows, second = first_inverse(pivot)
    panel = jnp.dot(inverse, kernel[:BLOCK], precision=HIGHEST)
    moved = regroup(panel.astype(jnp.bfloat16))
    lower = jnp.linalg.cholesky(second)
    identity = jnp.eye(BLOCK, dtype=jnp.float32)
    inverse = lax.linalg.triangular_solve(lower, identity, left_side=True, lower=True)
    residual = kernel[BLOCK:] - jnp.dot(prior_rows, panel, precision=HIGHEST)
    panel = jnp.dot(inverse, residual, precision=HIGHEST)
    results = [center_rows(moved, owned_count)]
    results.append(center_rows(regroup(panel.astype(jnp.bfloat16)), owned_count))
    return jnp.stack(results, axis=0)


def solution(mesh):
    placed = (P(("groups", "rows", "cols", "sub"), None), P("groups"))
    return jax.shard_map(
        local,
        mesh=mesh,
        in_specs=placed,
        out_specs=P("groups", ("rows", "cols", "sub"), None),
        check_vma=False,
    )
```
